32 devices in a mesh: seq: 8 (over z, y), head: 4 (over x, core).
Axes of the slice: x: 2, y: 2, z: 4, core: 2. Of those that a mesh axis runs over, the one named last changes fastest.
Arguments:
- vision: bfloat16 [16384, 7680], P(('seq', 'head')), may hold values from -6 to 6
- w_key: bfloat16 [7680, 512], replicated, may hold values from -0.0625 to 0.0625
- w_value: bfloat16 [7680, 512], replicated, may hold values from -0.0625 to 0.0625
- queries: bfloat16 [256, 4096], P('seq', 'head'), may hold values from -240 to 240
- w_out: bfloat16 [4096, 8192], P('head', 'seq'), may hold values from -0.09375 to 0.09375
Outputs:
- mixed: bfloat16 [256, 8192], P('head', 'seq')
The draws below stay inside these ranges and needn't reach their ends.
All inputs are finite; a program needn't handle non-finite values.
Results may differ from the reference program's by a relative error of at most 0.03.
Values may be sent and summed in bfloat16 or wider, within the bound.
A program may use at most 128 MiB of HBM per device.

```python
import jax
import jax.numpy as jnp
from jax import lax

VD = 7680
D = 8192
HD = 128
QH = 32
KV = 4
TEXT = 256
VTOK = 16384
N_SEQ = 8


def draw_queries(key, part):
    first_key = jax.random.fold_in(key, 11)
    base = jnp.clip(jax.random.normal(first_key, (TEXT, QH * HD), jnp.float32), -4.0, 4.0)
    result = base * 3.0
    return result.astype(jnp.bfloat16)


def steps_of(key, dims, shards, smallest, high):
    loudness, own = 1.0, jax.random.fold_in(key, 6)
    for axis_at, shards_of in shards:
        steps = jnp.exp(jax.random.uniform(jax.random.fold_in(own, axis_at), (shards_of,), jnp.float32, smallest / len(shards), high / len(shards)))
        loudness = loudness * jnp.repeat(steps, dims[axis_at] // shards_of).reshape([-1 if axis == axis_at else 1 for axis in range(len(dims))])
    return loudness


def noise(key, dims, deviation, bound, cuts=(), kind=jnp.bfloat16):
    entries = jax.random.normal(key, dims, jnp.float32) * deviation
    if len(cuts) > 0:
        entries = steps_of(key, dims, cuts, -0.22, 0.18) * entries
    return jnp.clip(entries, min=-bound, max=bound).astype(kind)


def setup_inputs(seed: int = 0) -> dict:
    seeds = jax.random.split(jax.random.key(seed), 6)
    vision = noise(seeds[0], (VTOK, VD), 1.0, 6.0, ((0, 32),))
    w_key = noise(seeds[1], (VD, KV * HD), VD ** -0.5, 0.0625)
    w_value = noise(seeds[2], (VD, KV * HD), VD ** -0.5, 0.0625)
    queries = draw_queries(jax.random.fold_in(seeds[5], 71), 0)
    w_out = noise(seeds[4], (QH * HD, D), (QH * HD) ** -0.5, 0.09375, ((0, 4), (1, 8)))
    return {"vision": vision, "w_key": w_key, "w_value": w_value, "queries": queries, "w_out": w_out}


def reference(vision, w_key, w_value, queries, w_out):
    keys = jnp.dot(vision, w_key, preferred_element_type=jnp.float32).astype(jnp.bfloat16)
    values = jnp.dot(vision, w_value, preferred_element_type=jnp.float32).astype(jnp.bfloat16)
    keys = lax.optimization_barrier(keys)
    values = lax.optimization_barrier(values)
    block_len = VTOK // N_SEQ
    group_size = QH // KV
    key_blocks = keys.reshape(N_SEQ, block_len, KV, HD)
    value_blocks = values.reshape(N_SEQ, block_len, KV, HD)
    grouped = queries.astype(jnp.float32).reshape(TEXT, KV, group_size, HD)

    def one_block(pair):
        key_part, value_part = pair
        scores = jnp.einsum("tkgd,nkd->kgtn", grouped, key_part.astype(jnp.float32)) * (HD ** -0.5)
        maxima = jnp.max(scores, axis=-1)
        powers = jnp.exp(scores - maxima[..., None])
        totals = jnp.sum(powers, axis=-1)
        rounded = lax.optimization_barrier(powers.astype(jnp.bfloat16))
        partial_value = jnp.einsum("kgtn,nkd->tkgd", rounded.astype(jnp.float32), value_part.astype(jnp.float32))
        partial_value = partial_value.reshape(TEXT, QH * HD)
        maxima = maxima.transpose(2, 0, 1).reshape(TEXT, QH)
        totals = totals.transpose(2, 0, 1).reshape(TEXT, QH)
        return maxima, totals, partial_value

    block_max, block_sum, block_out = lax.map(one_block, (key_blocks, value_blocks))
    row_max = jnp.max(block_max, axis=0)
    factor = jnp.exp(block_max - row_max[None])
    denom = jnp.sum(block_sum * factor, axis=0)
    numer = jnp.sum(block_out.reshape(N_SEQ, TEXT, QH, HD) * factor[..., None], axis=0)
    attended = (numer / denom[..., None]).reshape(TEXT, QH * HD).astype(jnp.bfloat16)
    return jnp.dot(attended, w_out, preferred_element_type=jnp.float32).astype(jnp.bfloat16)
```

```python
import functools
import math

import jax
import jax.numpy as jnp
from jax import lax
from jax.experimental import pallas as pl
from jax.experimental.pallas import tpu as pltpu
from jax.sharding import PartitionSpec as P

HD = 128
F32 = jnp.float32
BF16 = jnp.bfloat16
MESH = pl.DeviceIdType.MESH


def eye_mask(rows):
    return lax.broadcasted_iota(jnp.int32, (rows, HD), 0) == lax.broadcasted_iota(
        jnp.int32, (rows, HD), 1
    )


def to_rows(col, unit):
    part = min(unit, HD)
    eye = eye_mask(part)
    return [
        jnp.sum(jnp.where(eye, col[i * part : (i + 1) * part], 0.0), axis=0, keepdims=True)
        for i in range(unit // part)
    ]


def to_col(rows, unit):
    part = min(unit, HD)
    eye = eye_mask(part)
    parts = [
        jnp.sum(
            jnp.where(eye, jnp.broadcast_to(rows[i : i + 1], (part, HD)), 0.0),
            axis=1,
            keepdims=True,
        )
        for i in range(unit // part)
    ]
    return parts[0] if len(parts) == 1 else jnp.concatenate(parts, axis=0)


def kernel(
    n_s, n_h, n_c,
    vision, w_key, w_value, q, w_out, out,
    vbuf, wbuf, wobuf, acc, q_all, k_send, v_send, k_all, v_ext,
    o_near, m_near, o_send, s_send, o_recv, s_recv, a_send, a_full, r_send, r_recv,
    v_sem, wk_sem, wv_sem, wo_sem,
    q_ss, q_rs, k_ss, k_rs, vv_ss, vv_rs, o_ss, o_rs, s_ss, s_rs, a_ss, a_rs, r_ss, r_rs,
):
    me_s = lax.axis_index("seq")
    me_h = lax.axis_index("head")
    k_c = vbuf.shape[2]
    text_local = q.shape[0]
    heads = q.shape[1] // HD
    unit = text_local * heads
    per_head = n_s // heads
    half = n_h // 2
    n_rows = max(1, unit // HD)
    scale = math.log2(math.e) / math.sqrt(HD)

    def head_at(offset):
        return (lax.rem(me_h // 2 + offset // 2, half)) * 2 + lax.rem(
            lax.rem(me_h, 2) + lax.rem(offset, 2), 2
        )

    def head_from(offset):
        return (lax.rem(me_h // 2 + half - offset // 2, half)) * 2 + lax.rem(
            lax.rem(me_h, 2) + lax.rem(offset, 2), 2
        )

    def load_vision(c):
        return pltpu.make_async_copy(
            vision.at[:, pl.ds(pl.multiple_of(c * k_c, HD), k_c)], vbuf.at[c], v_sem.at[c]
        )

    def load_w(p, c):
        cols = pl.ds(pl.multiple_of(head_at(n_h - 1 - p) * HD, HD), HD)
        rows = pl.ds(pl.multiple_of(c * k_c, HD), k_c)
        return (
            pltpu.make_async_copy(
                w_key.at[rows, cols], wbuf.at[p, c, :, pl.ds(0, HD)], wk_sem.at[p, c]
            ),
            pltpu.make_async_copy(
                w_value.at[rows, cols], wbuf.at[p, c, :, pl.ds(HD, HD)], wv_sem.at[p, c]
            ),
        )

    def start_w(p, c):
        for copy in load_w(p, c):
            copy.start()

    def wait_w(p, c):
        for copy in load_w(p, c):
            copy.wait()

    def first_loads(c, carry):
        load_vision(c).start()
        start_w(0, c)
        return carry

    lax.fori_loop(0, n_c, first_loads, 0)

    barrier = pltpu.get_barrier_semaphore()

    def greet_seq(i, carry):
        pl.semaphore_signal(
            barrier, inc=1, device_id=(lax.rem(me_s + i, n_s), me_h), device_id_type=MESH
        )
        return carry

    def greet_head(i, carry):
        pl.semaphore_signal(
            barrier, inc=1, device_id=(me_s, lax.rem(me_h + i, n_h)), device_id_type=MESH
        )
        return carry

    lax.fori_loop(1, n_s, greet_seq, 0)
    lax.fori_loop(1, n_h, greet_head, 0)
    v_ext[:, :, HD:] = jnp.ones((n_h, v_ext.shape[1], HD), BF16)
    q_all[me_s] = q[...]
    pl.semaphore_wait(barrier, n_s + n_h - 2)

    def q_copy(to, slot, i):
        return pltpu.make_async_remote_copy(
            src_ref=q, dst_ref=q_all.at[slot], send_sem=q_ss.at[i], recv_sem=q_rs.at[i],
            device_id=(to, me_h), device_id_type=MESH,
        )

    def q_start(i, carry):
        q_copy(lax.rem(me_s + i, n_s), me_s, i).start()
        return carry

    lax.fori_loop(1, n_s, q_start, 0)

    def kv_copies(offset, to):
        return (
            pltpu.make_async_remote_copy(
                src_ref=k_send.at[offset], dst_ref=k_all.at[offset],
                send_sem=k_ss.at[offset], recv_sem=k_rs.at[offset],
                device_id=(me_s, to), device_id_type=MESH,
            ),
            pltpu.make_async_remote_copy(
                src_ref=v_send.at[offset], dst_ref=v_ext.at[offset, :, pl.ds(0, HD)],
                send_sem=vv_ss.at[offset], recv_sem=vv_rs.at[offset],
                device_id=(me_s, to), device_id_type=MESH,
            ),
        )

    for p in range(n_h):
        offset = n_h - 1 - p

        def chunk(c, carry, p=p):
            if p == 0:
                load_vision(c).wait()
            wait_w(p, c)
            if p + 1 < n_h:
                start_w(p + 1, c)
            got = jnp.dot(vbuf[c], wbuf[p, c], preferred_element_type=F32)

            @pl.when(c == 0)
            def _():
                acc[...] = got

            @pl.when(c > 0)
            def _():
                acc[...] += got

            return carry

        lax.fori_loop(0, n_c, chunk, 0)
        if offset:
            k_send[offset] = acc[:, :HD].astype(BF16)
            v_send[offset] = acc[:, HD:].astype(BF16)
            for copy in kv_copies(offset, head_at(offset)):
                copy.start()
        else:
            k_all[0] = acc[:, :HD].astype(BF16)
            v_ext[0, :, :HD] = acc[:, HD:].astype(BF16)

    load_out = pltpu.make_async_copy(w_out, wobuf, wo_sem)
    load_out.start()

    def q_wait(i, carry):
        q_copy(lax.rem(me_s + i, n_s), lax.rem(me_s + n_s - i, n_s), i).wait_recv()
        return carry

    lax.fori_loop(1, n_s, q_wait, 0)

    def block(u, first, last):
        col = pl.ds(pl.multiple_of((u // per_head) * HD, HD), HD)
        rows = pl.ds(0, heads) if per_head == 1 else pl.ds(lax.rem(u, per_head) * heads, heads)
        qv = q_all[rows, :, col].reshape(unit, HD)
        k = k_all[first:last].reshape(-1, HD)
        v = v_ext[first:last].reshape(-1, 2 * HD)
        s = lax.dot_general(qv, k, (((1,), (1,)), ((), ())), preferred_element_type=F32)
        m = jnp.max(s, axis=1, keepdims=True)
        w = jnp.exp2((s - m) * scale).astype(BF16)
        return jnp.dot(w, v, preferred_element_type=F32), jnp.broadcast_to(m, (unit, HD))

    for offset in range(1, half):
        for copy in kv_copies(offset, head_from(offset)):
            copy.wait_recv()

    def near(i, carry):
        o, m = block(lax.rem(me_s + 1 + i, n_s), 0, half)
        o_near[i] = o
        m_near[i] = m
        return carry

    lax.fori_loop(0, n_s, near, 0)

    for offset in range(half, n_h):
        for copy in kv_copies(offset, head_from(offset)):
            copy.wait_recv()

    def o_copies(i, to, slot):
        return (
            pltpu.make_async_remote_copy(
                src_ref=o_send.at[i], dst_ref=o_recv.at[slot],
                send_sem=o_ss.at[i], recv_sem=o_rs.at[i],
                device_id=(to, me_h), device_id_type=MESH,
            ),
            pltpu.make_async_remote_copy(
                src_ref=s_send.at[i], dst_ref=s_recv.at[slot],
                send_sem=s_ss.at[i], recv_sem=s_rs.at[i],
                device_id=(to, me_h), device_id_type=MESH,
            ),
        )

    def far_block(i, u):
        o2, m2 = block(u, half, n_h)
        o1, m1 = o_near[i], m_near[i]
        m = jnp.maximum(m1, m2)
        e1 = jnp.exp2((m1 - m) * scale)
        e2 = jnp.exp2((m2 - m) * scale)
        numer = o1[:, :HD] * e1 + o2[:, :HD] * e2
        total = o1[:, HD:] * e1 + o2[:, HD:] * e2
        return numer.astype(BF16), to_rows(m, unit), to_rows(total, unit)

    def far(i, carry):
        u = lax.rem(me_s + 1 + i, n_s)
        numer, m_rows, t_rows = far_block(i, u)
        o_send[i] = numer
        for r in range(n_rows):
            s_send[i, r : r + 1] = m_rows[r]
            s_send[i, n_rows + r : n_rows + r + 1] = t_rows[r]
        for copy in o_copies(i, u, me_s):
            copy.start()
        return carry

    lax.fori_loop(0, n_s - 1, far, 0)
    numer, m_rows, t_rows = far_block(n_s - 1, me_s)
    o_recv[me_s] = numer
    for r in range(n_rows):
        s_recv[me_s, r : r + 1] = m_rows[r]
        s_recv[me_s, n_rows + r : n_rows + r + 1] = t_rows[r]

    def o_wait(i, carry):
        for copy in o_copies(i, lax.rem(me_s + 1 + i, n_s), lax.rem(me_s + n_s - 1 - i, n_s)):
            copy.wait_recv()
        return carry

    lax.fori_loop(0, n_s - 1, o_wait, 0)
    m_all = s_recv[:, 0:n_rows]
    m_top = jnp.max(m_all, axis=0, keepdims=True)
    e_all = jnp.exp2((m_all - m_top) * scale)
    f_all = e_all / jnp.sum(e_all * s_recv[:, n_rows : 2 * n_rows], axis=0, keepdims=True)
    att = jnp.zeros((unit, HD), F32)
    for b in range(n_s):
        att += to_col(f_all[b], unit) * o_recv[b].astype(F32)
    a_send[...] = att.astype(BF16)

    def place(u):
        rows = (
            pl.ds(0, unit)
            if per_head == 1
            else pl.ds(pl.multiple_of(lax.rem(u, per_head) * unit, 16), unit)
        )
        return rows, pl.ds(pl.multiple_of((u // per_head) * HD, HD), HD)

    def a_copy(i, to, u):
        rows, cols = place(u)
        return pltpu.make_async_remote_copy(
            src_ref=a_send, dst_ref=a_full.at[rows, cols],
            send_sem=a_ss.at[i], recv_sem=a_rs.at[i],
            device_id=(to, me_h), device_id_type=MESH,
        )

    def a_start(i, carry):
        a_copy(i, lax.rem(me_s + i, n_s), me_s).start()
        return carry

    def a_wait(i, carry):
        a_copy(i, lax.rem(me_s + i, n_s), lax.rem(me_s + n_s - i, n_s)).wait_recv()
        return carry

    lax.fori_loop(1, n_s, a_start, 0)
    rows, cols = place(me_s)
    a_full[rows, cols] = a_send[...]
    load_out.wait()
    lax.fori_loop(1, n_s, a_wait, 0)

    share = jnp.dot(a_full[...], wobuf[...], preferred_element_type=F32)
    r_send[...] = share.astype(BF16).reshape(r_send.shape)

    def r_copy(offset, to):
        return pltpu.make_async_remote_copy(
            src_ref=r_send.at[to], dst_ref=r_recv.at[offset],
            send_sem=r_ss.at[offset], recv_sem=r_rs.at[offset],
            device_id=(me_s, to), device_id_type=MESH,
        )

    for offset in range(n_h - 1, 0, -1):
        r_copy(offset, head_at(offset)).start()
    total = r_send[me_h].astype(F32)
    for offset in range(1, n_h):
        r_copy(offset, head_from(offset)).wait_recv()
        total += r_recv[offset].astype(F32)
    out[...] = total.astype(BF16)

    def q_sent(i, carry):
        q_copy(lax.rem(me_s + i, n_s), me_s, i).wait_send()
        a_copy(i, lax.rem(me_s + i, n_s), me_s).wait_send()
        return carry

    def o_sent(i, carry):
        for copy in o_copies(i, lax.rem(me_s + 1 + i, n_s), me_s):
            copy.wait_send()
        return carry

    lax.fori_loop(1, n_s, q_sent, 0)
    lax.fori_loop(0, n_s - 1, o_sent, 0)
    for offset in range(1, n_h):
        for copy in kv_copies(offset, head_at(offset)):
            copy.wait_send()
        r_copy(offset, head_at(offset)).wait_send()


def shards(n_s, n_h, vision, w_key, w_value, queries, w_out):
    tokens, width = vision.shape
    text_local, features = queries.shape
    heads = features // HD
    text = text_local * n_s
    unit = text_local * heads
    out_cols = w_out.shape[1]
    n_c = max(d for d in range(1, 7) if width % (d * HD) == 0)
    k_c = width // n_c
    vmem = pltpu.VMEM
    dma = pltpu.SemaphoreType.DMA
    scratch = [
        vmem((n_c, tokens, k_c), BF16),
        vmem((n_h, n_c, k_c, 2 * HD), BF16),
        vmem(w_out.shape, BF16),
        vmem((tokens, 2 * HD), F32),
        vmem((n_s, text_local, features), BF16),
        vmem((n_h, tokens, HD), BF16),
        vmem((n_h, tokens, HD), BF16),
        vmem((n_h, tokens, HD), BF16),
        vmem((n_h, tokens, 2 * HD), BF16),
        vmem((n_s, unit, 2 * HD), F32),
        vmem((n_s, unit, HD), F32),
        vmem((n_s, unit, HD), BF16),
        vmem((n_s, 8, HD), F32),
        vmem((n_s, unit, HD), BF16),
        vmem((n_s, 8, HD), F32),
        vmem((unit, HD), BF16),
        vmem((text, features), BF16),
        vmem((n_h, text // n_h, out_cols), BF16),
        vmem((n_h, text // n_h, out_cols), BF16),
        dma((n_c,)), dma((n_h, n_c)), dma((n_h, n_c)), dma,
        dma((n_s,)), dma((n_s,)),
        dma((n_h,)), dma((n_h,)), dma((n_h,)), dma((n_h,)),
        dma((n_s,)), dma((n_s,)), dma((n_s,)), dma((n_s,)),
        dma((n_s,)), dma((n_s,)),
        dma((n_h,)), dma((n_h,)),
    ]
    anywhere = pl.BlockSpec(memory_space=pl.ANY)
    inside = pl.BlockSpec(memory_space=pltpu.VMEM)
    return pl.pallas_call(
        functools.partial(kernel, n_s, n_h, n_c),
        out_shape=jax.ShapeDtypeStruct((text // n_h, out_cols), BF16),
        in_specs=[anywhere, anywhere, anywhere, inside, anywhere],
        out_specs=inside,
        scratch_shapes=scratch,
        compiler_params=pltpu.CompilerParams(
            collective_id=0, has_side_effects=True, vmem_limit_bytes=56 * 1024 * 1024
        ),
    )(vision, w_key, w_value, queries, w_out)


def solution(mesh):
    placed = (P(("seq", "head"), None), P(), P(), P("seq", "head"), P("head", "seq"))
    return jax.shard_map(
        functools.partial(shards, mesh.shape["seq"], mesh.shape["head"]),
        mesh=mesh, in_specs=placed, out_specs=P("head", "seq"), check_vma=False,
    )
```

```python
import functools
import math

import jax
import jax.numpy as jnp
from jax import lax
from jax.experimental import pallas as pl
from jax.experimental.pallas import tpu as pltpu
from jax.sharding import PartitionSpec as P

HD = 128
F32 = jnp.float32
BF16 = jnp.bfloat16
MESH = pl.DeviceIdType.MESH


def eye_mask(rows):
    return lax.broadcasted_iota(jnp.int32, (rows, HD), 0) == lax.broadcasted_iota(
        jnp.int32, (rows, HD), 1
    )


def to_rows(col, unit):
    part = min(unit, HD)
    eye = eye_mask(part)
    return [
        jnp.sum(jnp.where(eye, col[i * part : (i + 1) * part], 0.0), axis=0, keepdims=True)
        for i in range(unit // part)
    ]


def to_col(rows, unit):
    part = min(unit, HD)
    eye = eye_mask(part)
    parts = [
        jnp.sum(
            jnp.where(eye, jnp.broadcast_to(rows[i : i + 1], (part, HD)), 0.0),
            axis=1,
            keepdims=True,
        )
        for i in range(unit // part)
    ]
    return parts[0] if len(parts) == 1 else jnp.concatenate(parts, axis=0)


def kernel(
    n_s, n_h, n_c,
    vision, w_key, w_value, q, w_out, out,
    vbuf, wbuf, wobuf, acc, q_all, k_send, v_send, k_all, v_ext,
    o_near, m_near, p_send, t_send, p_recv, t_recv, o_send, s_send, o_recv, s_recv, a_send, a_full, r_send, r_recv,
    v_sem, wk_sem, wv_sem, wo_sem,
    q_ss, q_rs, k_ss, k_rs, vv_ss, vv_rs, p_ss, p_rs, t_ss, t_rs,
    o_ss, o_rs, s_ss, s_rs, a_ss, a_rs, f_ss, f_rs, r_ss, r_rs,
):
    me_s = lax.axis_index("seq")
    me_h = lax.axis_index("head")
    k_c = vbuf.shape[2]
    text_local = q.shape[0]
    heads = q.shape[1] // HD
    unit = text_local * heads
    per_head = n_s // heads
    half = n_h // 2
    n_rows = max(1, unit // HD)
    scale = math.log2(math.e) / math.sqrt(HD)

    def head_at(offset):
        return (lax.rem(me_h // 2 + offset // 2, half)) * 2 + lax.rem(
            lax.rem(me_h, 2) + lax.rem(offset, 2), 2
        )

    def head_from(offset):
        return (lax.rem(me_h // 2 + half - offset // 2, half)) * 2 + lax.rem(
            lax.rem(me_h, 2) + lax.rem(offset, 2), 2
        )

    def load_vision(c):
        return pltpu.make_async_copy(
            vision.at[:, pl.ds(pl.multiple_of(c * k_c, HD), k_c)], vbuf.at[c], v_sem.at[c]
        )

    def load_w(p, c):
        cols = pl.ds(pl.multiple_of(head_at(n_h - 1 - p) * HD, HD), HD)
        rows = pl.ds(pl.multiple_of(c * k_c, HD), k_c)
        return (
            pltpu.make_async_copy(
                w_key.at[rows, cols], wbuf.at[p, c, :, pl.ds(0, HD)], wk_sem.at[p, c]
            ),
            pltpu.make_async_copy(
                w_value.at[rows, cols], wbuf.at[p, c, :, pl.ds(HD, HD)], wv_sem.at[p, c]
            ),
        )

    def start_w(p, c):
        for copy in load_w(p, c):
            copy.start()

    def wait_w(p, c):
        for copy in load_w(p, c):
            copy.wait()

    def first_loads(c, carry):
        load_vision(c).start()
        start_w(0, c)
        return carry

    lax.fori_loop(0, n_c, first_loads, 0)

    barrier = pltpu.get_barrier_semaphore()

    def greet_seq(i, carry):
        pl.semaphore_signal(
            barrier, inc=1, device_id=(lax.rem(me_s + i, n_s), me_h), device_id_type=MESH
        )
        return carry

    def greet_head(i, carry):
        pl.semaphore_signal(
            barrier, inc=1, device_id=(me_s, lax.rem(me_h + i, n_h)), device_id_type=MESH
        )
        return carry

    lax.fori_loop(1, n_s, greet_seq, 0)
    lax.fori_loop(1, n_h, greet_head, 0)
    v_ext[:, :, HD:] = jnp.ones((n_h, v_ext.shape[1], HD), BF16)
    q_all[me_s] = q[...]
    pl.semaphore_wait(barrier, n_s + n_h - 2)

    def q_copy(to, slot, i):
        return pltpu.make_async_remote_copy(
            src_ref=q, dst_ref=q_all.at[slot], send_sem=q_ss.at[i], recv_sem=q_rs.at[i],
            device_id=(to, me_h), device_id_type=MESH,
        )

    def q_start(i, carry):
        q_copy(lax.rem(me_s + i, n_s), me_s, i).start()
        return carry

    lax.fori_loop(1, n_s, q_start, 0)

    def kv_copies(offset, to):
        return (
            pltpu.make_async_remote_copy(
                src_ref=k_send.at[offset], dst_ref=k_all.at[offset],
                send_sem=k_ss.at[offset], recv_sem=k_rs.at[offset],
                device_id=(me_s, to), device_id_type=MESH,
            ),
            pltpu.make_async_remote_copy(
                src_ref=v_send.at[offset], dst_ref=v_ext.at[offset, :, pl.ds(0, HD)],
                send_sem=vv_ss.at[offset], recv_sem=vv_rs.at[offset],
                device_id=(me_s, to), device_id_type=MESH,
            ),
        )

    for p in range(n_h):
        offset = n_h - 1 - p

        def chunk(c, carry, p=p):
            if p == 0:
                load_vision(c).wait()
            wait_w(p, c)
            if p + 1 < n_h:
                start_w(p + 1, c)
            got = jnp.dot(vbuf[c], wbuf[p, c], preferred_element_type=F32)

            @pl.when(c == 0)
            def _():
                acc[...] = got

            @pl.when(c > 0)
            def _():
                acc[...] += got

            return carry

        lax.fori_loop(0, n_c, chunk, 0)
        if offset:
            k_send[offset] = acc[:, :HD].astype(BF16)
            v_send[offset] = acc[:, HD:].astype(BF16)
            for copy in kv_copies(offset, head_at(offset)):
                copy.start()
        else:
            k_all[0] = acc[:, :HD].astype(BF16)
            v_ext[0, :, :HD] = acc[:, HD:].astype(BF16)

    load_out = pltpu.make_async_copy(w_out, wobuf, wo_sem)
    load_out.start()

    def q_wait(i, carry):
        q_copy(lax.rem(me_s + i, n_s), lax.rem(me_s + n_s - i, n_s), i).wait_recv()
        return carry

    lax.fori_loop(1, n_s, q_wait, 0)

    def block(u, first, last):
        col = pl.ds(pl.multiple_of((u // per_head) * HD, HD), HD)
        rows = pl.ds(0, heads) if per_head == 1 else pl.ds(lax.rem(u, per_head) * heads, heads)
        qv = q_all[rows, :, col].reshape(unit, HD)
        k = k_all[first:last].reshape(-1, HD)
        v = v_ext[first:last].reshape(-1, 2 * HD)
        s = lax.dot_general(qv, k, (((1,), (1,)), ((), ())), preferred_element_type=F32)
        m = jnp.max(s, axis=1, keepdims=True)
        w = jnp.exp2((s - m) * scale).astype(BF16)
        return jnp.dot(w, v, preferred_element_type=F32), jnp.broadcast_to(m, (unit, HD))

    for offset in range(1, half):
        for copy in kv_copies(offset, head_from(offset)):
            copy.wait_recv()

    n_a = n_s // 2
    me_a, me_b = me_s // 2, lax.rem(me_s, 2)
    pair = 2 * me_a + 1 - me_b

    def major(j):
        return lax.rem(me_a + 1 + j, n_a)

    def near(j, carry):
        first = block(2 * major(j) + 1 - me_b, 0, half)
        second = block(2 * major(j) + me_b, 0, half)
        o_near[j], m_near[j] = first
        o_near[n_a + j], m_near[n_a + j] = second
        return carry

    lax.fori_loop(0, n_a, near, 0)

    for offset in range(half, n_h):
        for copy in kv_copies(offset, head_from(offset)):
            copy.wait_recv()

    def p_copies(j):
        return (
            pltpu.make_async_remote_copy(
                src_ref=p_send.at[j], dst_ref=p_recv.at[j],
                send_sem=p_ss.at[j], recv_sem=p_rs.at[j],
                device_id=(pair, me_h), device_id_type=MESH,
            ),
            pltpu.make_async_remote_copy(
                src_ref=t_send.at[j], dst_ref=t_recv.at[j],
                send_sem=t_ss.at[j], recv_sem=t_rs.at[j],
                device_id=(pair, me_h), device_id_type=MESH,
            ),
        )

    def o_copies(j, to_a, slot):
        return (
            pltpu.make_async_remote_copy(
                src_ref=o_send.at[j], dst_ref=o_recv.at[slot],
                send_sem=o_ss.at[j], recv_sem=o_rs.at[j],
                device_id=(2 * to_a + me_b, me_h), device_id_type=MESH,
            ),
            pltpu.make_async_remote_copy(
                src_ref=s_send.at[j], dst_ref=s_recv.at[slot],
                send_sem=s_ss.at[j], recv_sem=s_rs.at[j],
                device_id=(2 * to_a + me_b, me_h), device_id_type=MESH,
            ),
        )

    def put_stats(ref, at, m, total):
        m_rows, t_rows = to_rows(m, unit), to_rows(total, unit)
        for r in range(n_rows):
            ref[at, r : r + 1] = m_rows[r]
            ref[at, n_rows + r : n_rows + r + 1] = t_rows[r]

    def far_pair(j, carry):
        o2, m2 = block(2 * major(j) + 1 - me_b, half, n_h)
        o1, m1 = o_near[j], m_near[j]
        m = jnp.maximum(m1, m2)
        e1 = jnp.exp2((m1 - m) * scale)
        e2 = jnp.exp2((m2 - m) * scale)
        p_send[j] = (o1[:, :HD] * e1 + o2[:, :HD] * e2).astype(BF16)
        put_stats(t_send, j, m, o1[:, HD:] * e1 + o2[:, HD:] * e2)
        for copy in p_copies(j):
            copy.start()
        return carry

    lax.fori_loop(0, n_a, far_pair, 0)

    def far_own(j):
        o2, m2 = block(2 * major(j) + me_b, half, n_h)
        for copy in p_copies(j):
            copy.wait_recv()
        o1, m1 = o_near[n_a + j], m_near[n_a + j]
        m3 = to_col(t_recv[j, 0:n_rows], unit)
        t3 = to_col(t_recv[j, n_rows : 2 * n_rows], unit)
        m = jnp.maximum(jnp.maximum(m1, m2), m3)
        e1 = jnp.exp2((m1 - m) * scale)
        e2 = jnp.exp2((m2 - m) * scale)
        e3 = jnp.exp2((m3 - m) * scale)
        numer = o1[:, :HD] * e1 + o2[:, :HD] * e2 + p_recv[j].astype(F32) * e3
        return numer.astype(BF16), m, o1[:, HD:] * e1 + o2[:, HD:] * e2 + t3 * e3

    def far(j, carry):
        numer, m, total = far_own(j)
        o_send[j] = numer
        put_stats(s_send, j, m, total)
        for copy in o_copies(j, major(j), me_a):
            copy.start()
        return carry

    lax.fori_loop(0, n_a - 1, far, 0)
    numer, m, total = far_own(n_a - 1)
    o_recv[me_a] = numer
    put_stats(s_recv, me_a, m, total)

    def o_wait(j, carry):
        for copy in o_copies(j, major(j), lax.rem(me_a + n_a - 1 - j, n_a)):
            copy.wait_recv()
        return carry

    lax.fori_loop(0, n_a - 1, o_wait, 0)
    m_all = s_recv[:, 0:n_rows]
    m_top = jnp.max(m_all, axis=0, keepdims=True)
    e_all = jnp.exp2((m_all - m_top) * scale)
    f_all = e_all / jnp.sum(e_all * s_recv[:, n_rows : 2 * n_rows], axis=0, keepdims=True)
    att = jnp.zeros((unit, HD), F32)
    for b in range(n_a):
        att += to_col(f_all[b], unit) * o_recv[b].astype(F32)

    part = r_send.shape[2]
    att = att.reshape(unit // (2 * part), 2, part, HD)
    rows_here = unit // 2

    def place(h, u):
        rows = (
            pl.ds(0, rows_here)
            if per_head == 1
            else pl.ds(pl.multiple_of(lax.rem(u, per_head) * rows_here, 16), rows_here)
        )
        return h, rows, pl.ds(pl.multiple_of((u // per_head) * HD, HD), HD)

    def a_copy(h, i, to, u):
        return pltpu.make_async_remote_copy(
            src_ref=a_send.at[h], dst_ref=a_full.at[place(h, u)],
            send_sem=a_ss.at[h, i], recv_sem=a_rs.at[h, i],
            device_id=(to, me_h), device_id_type=MESH,
        )

    def f_copy(h, i, u):
        return pltpu.make_async_remote_copy(
            src_ref=a_full.at[place(h, u)], dst_ref=a_full.at[place(h, u)],
            send_sem=f_ss.at[h, i], recv_sem=f_rs.at[h, i],
            device_id=(pair, me_h), device_id_type=MESH,
        )

    def r_copy(h, offset, to):
        return pltpu.make_async_remote_copy(
            src_ref=r_send.at[h, to], dst_ref=r_recv.at[h, offset],
            send_sem=r_ss.at[h, offset], recv_sem=r_rs.at[h, offset],
            device_id=(me_s, to), device_id_type=MESH,
        )

    def ahead(i):
        return 2 * lax.rem(me_a + i, n_a)

    def behind(i):
        return 2 * lax.rem(me_a + n_a - i, n_a)

    for h in range(2):
        a_send[h] = att[:, h].reshape(rows_here, HD).astype(BF16)

        def a_start(i, carry, h=h):
            a_copy(h, i, ahead(i) + me_b, me_s).start()
            return carry

        a_copy(h, 0, pair, me_s).start()
        lax.fori_loop(1, n_a, a_start, 0)
        a_full[place(h, me_s)] = a_send[h]

    load_out.wait()
    for h in range(2):

        def forward(i, carry, h=h):
            a_copy(h, i, ahead(i) + me_b, behind(i) + me_b).wait_recv()
            f_copy(h, i, behind(i) + me_b).start()
            return carry

        def forwarded(i, carry, h=h):
            f_copy(h, i, behind(i) + 1 - me_b).wait_recv()
            return carry

        lax.fori_loop(1, n_a, forward, 0)
        a_copy(h, 0, pair, pair).wait_recv()
        lax.fori_loop(1, n_a, forwarded, 0)
        share = jnp.dot(a_full[h], wobuf[...], preferred_element_type=F32)
        r_send[h] = share.astype(BF16).reshape(n_h, part, -1)
        for offset in range(n_h - 1, 0, -1):
            r_copy(h, offset, head_at(offset)).start()

    for h in range(2):
        total = r_send[h, me_h].astype(F32)
        for offset in range(1, n_h):
            r_copy(h, offset, head_from(offset)).wait_recv()
            total += r_recv[h, offset].astype(F32)
        out[h * part : (h + 1) * part] = total.astype(BF16)

    def q_sent(i, carry):
        q_copy(lax.rem(me_s + i, n_s), me_s, i).wait_send()
        return carry

    def p_sent(j, carry):
        for copy in p_copies(j):
            copy.wait_send()
        return carry

    def o_sent(j, carry):
        for copy in o_copies(j, major(j), me_a):
            copy.wait_send()
        return carry

    lax.fori_loop(1, n_s, q_sent, 0)
    lax.fori_loop(0, n_a, p_sent, 0)
    lax.fori_loop(0, n_a - 1, o_sent, 0)
    for offset in range(1, n_h):
        for copy in kv_copies(offset, head_at(offset)):
            copy.wait_send()
    for h in range(2):
        a_copy(h, 0, pair, me_s).wait_send()

        def a_sent(i, carry, h=h):
            a_copy(h, i, ahead(i) + me_b, me_s).wait_send()
            f_copy(h, i, behind(i) + me_b).wait_send()
            return carry

        lax.fori_loop(1, n_a, a_sent, 0)
        for offset in range(1, n_h):
            r_copy(h, offset, head_at(offset)).wait_send()


def shards(n_s, n_h, vision, w_key, w_value, queries, w_out):
    tokens, width = vision.shape
    text_local, features = queries.shape
    heads = features // HD
    text = text_local * n_s
    unit = text_local * heads
    n_a = n_s // 2
    out_cols = w_out.shape[1]
    n_c = max(d for d in range(1, 7) if width % (d * HD) == 0)
    k_c = width // n_c
    vmem = pltpu.VMEM
    dma = pltpu.SemaphoreType.DMA
    scratch = [
        vmem((n_c, tokens, k_c), BF16),
        vmem((n_h, n_c, k_c, 2 * HD), BF16),
        vmem(w_out.shape, BF16),
        vmem((tokens, 2 * HD), F32),
        vmem((n_s, text_local, features), BF16),
        vmem((n_h, tokens, HD), BF16),
        vmem((n_h, tokens, HD), BF16),
        vmem((n_h, tokens, HD), BF16),
        vmem((n_h, tokens, 2 * HD), BF16),
        vmem((n_s, unit, 2 * HD), F32),
        vmem((n_s, unit, HD), F32),
        vmem((n_a, unit, HD), BF16),
        vmem((n_a, 8, HD), F32),
        vmem((n_a, unit, HD), BF16),
        vmem((n_a, 8, HD), F32),
        vmem((n_a, unit, HD), BF16),
        vmem((n_a, 8, HD), F32),
        vmem((n_a, unit, HD), BF16),
        vmem((n_a, 8, HD), F32),
        vmem((2, unit // 2, HD), BF16),
        vmem((2, text // 2, features), BF16),
        vmem((2, n_h, text // n_h // 2, out_cols), BF16),
        vmem((2, n_h, text // n_h // 2, out_cols), BF16),
        dma((n_c,)), dma((n_h, n_c)), dma((n_h, n_c)), dma,
        dma((n_s,)), dma((n_s,)),
        dma((n_h,)), dma((n_h,)), dma((n_h,)), dma((n_h,)),
        dma((n_a,)), dma((n_a,)), dma((n_a,)), dma((n_a,)),
        dma((n_a,)), dma((n_a,)), dma((n_a,)), dma((n_a,)),
        dma((2, n_a)), dma((2, n_a)), dma((2, n_a)), dma((2, n_a)),
        dma((2, n_h)), dma((2, n_h)),
    ]
    anywhere = pl.BlockSpec(memory_space=pl.ANY)
    inside = pl.BlockSpec(memory_space=pltpu.VMEM)
    return pl.pallas_call(
        functools.partial(kernel, n_s, n_h, n_c),
        out_shape=jax.ShapeDtypeStruct((text // n_h, out_cols), BF16),
        in_specs=[anywhere, anywhere, anywhere, inside, anywhere],
        out_specs=inside,
        scratch_shapes=scratch,
        compiler_params=pltpu.CompilerParams(
            collective_id=0, has_side_effects=True, vmem_limit_bytes=56 * 1024 * 1024
        ),
    )(vision, w_key, w_value, queries, w_out)


def solution(mesh):
    placed = (P(("seq", "head"), None), P(), P(), P("seq", "head"), P("head", "seq"))
    return jax.shard_map(
        functools.partial(shards, mesh.shape["seq"], mesh.shape["head"]),
        mesh=mesh, in_specs=placed, out_specs=P("head", "seq"), check_vma=False,
    )
```
